768 devices in a mesh: ctx: 96 (over z, x, core), exp: 8 (over y).
Axes of the slice: x: 4, y: 8, z: 12, core: 2. Of those that a mesh axis runs over, the one named last changes fastest.
Arguments:
- ssd_grad: bfloat16 [98304, 4096], P('ctx', 'exp'), may hold values from -6 to 6
- in_proj_b: bfloat16 [98304, 128], P('ctx'), may hold values from -0.1796875 to 0.1796875
- in_proj_c: bfloat16 [98304, 128], P('ctx'), may hold values from -0.1796875 to 0.1796875
- log_decay: float32 [64, 98304], P('exp', 'ctx'), may hold values from -1 to 0
- expert_grad: bfloat16 [98304, 4096], P(('ctx', 'exp')), may hold values from -6 to 6
- route: int32 [98304, 1], P(('ctx', 'exp')), may hold values from 0 to 7; in each aligned block of 128 rows (0 to 127, 128 to 255, ...) at most 24 rows name the same one
- gate_prob: float32 [98304], P(('ctx', 'exp')), may hold values from 0.1 to 1
- down_weight: bfloat16 [8, 768, 4096], P('exp'), may hold values from -0.21875 to 0.21875
- saved_pre: bfloat16 [96, 8, 8, 24, 1536], P('ctx', 'exp'), may hold values from -6 to 6
Outputs:
- input_grad: bfloat16 [98304, 4096], P('ctx', 'exp')
- pre_grad: bfloat16 [96, 8, 8, 24, 1536], P('ctx', 'exp')
The draws below stay inside these ranges and needn't reach their ends.
Inputs may be any that keep to these rules, and one draw needn't show every extreme that they name: `route`: in each aligned block of 128 rows no expert is named by more than 24 rows.
All inputs are finite; a program needn't handle non-finite values.
Results may differ from the reference program's by a relative error of at most 0.0051.
Values may be sent and summed in bfloat16 or wider, within the bound.
A program may use at most 128 MiB of HBM per device.

```python
import math
import jax
import jax.numpy as jnp
import numpy as np
from jax import lax

D = 4096
FF = 768
MIXER_HEADS = 64
HEAD_DIM = 64
STATE = 128
BLOCK = 256
BLOCKS_DEV = 4
SEQUENCE_TOKENS = 98304
TOK_DEV = 128
CAP = 24
N_CTX = 96
N_EXP = 8


def draw_log_decay(key, part):
    key = jax.random.fold_in(key, 7)
    random_keys = jax.random.split(key, 7)
    fast_head = jax.random.randint(random_keys[0], (MIXER_HEADS, 1, 1), 0, 2) == 1
    fast_rate = jax.random.uniform(random_keys[1], (MIXER_HEADS, 1, 1), jnp.float32, 0.02, 0.033)
    slow_rate = jax.random.uniform(random_keys[2], (MIXER_HEADS, 1, 1), jnp.float32, 0.1, 0.4) / SEQUENCE_TOKENS
    step_rate = jnp.where(fast_head, fast_rate, slow_rate)
    device_rows = BLOCK * BLOCKS_DEV
    groups = SEQUENCE_TOKENS // device_rows
    group_factor = jnp.exp(jax.random.uniform(random_keys[3], (MIXER_HEADS, groups, 1), jnp.float32, math.log(0.7), math.log(1.4)))
    token_factor = jax.random.uniform(random_keys[4], (MIXER_HEADS, groups, device_rows), jnp.float32, 0.5, 1.5)
    base_offset = -(step_rate * group_factor * token_factor).reshape(MIXER_HEADS, SEQUENCE_TOKENS)
    token_positions = jax.random.randint(random_keys[5], (3,), 0, SEQUENCE_TOKENS)
    spike_mask = jnp.any(jnp.arange(SEQUENCE_TOKENS)[None, :] == token_positions[:, None], axis=0)
    spike_loss = jax.random.uniform(random_keys[6], (MIXER_HEADS, 1), jnp.float32, 0.2, 0.4)
    return base_offset + jnp.where(spike_mask[None, :], jnp.log1p(-spike_loss), 0.0)


def shard_levels(own_key, dims, cuts, least, high):
    gain, own = 1.0, jax.random.fold_in(own_key, 6)
    for axis_at, parts in cuts:
        draws = jnp.exp(jax.random.uniform(jax.random.fold_in(own, axis_at), (parts,), jnp.float32, least / len(cuts), high / len(cuts)))
        gain = gain * jnp.repeat(draws, dims[axis_at] // parts).reshape([-1 if axis == axis_at else 1 for axis in range(len(dims))])
    return gain


def shared_out(key, own, number, rows, amount, top, bound, lean):
    sequence = jax.random.permutation(key, amount)
    heavy_load, usual = portions_of(amount, rows * top, bound, lean, True), portions_of(amount, rows * top, bound, lean, False)
    places = jnp.arange(amount)

    def named(lengths, offset_by):
        used = int((lengths > 0).sum())
        fixed = max(1, used // 4)
        passed = fixed + (places - fixed + offset_by * (used - fixed)) % max(1, amount - fixed)
        return jnp.zeros((amount,), jnp.int32).at[sequence[jnp.where(places < fixed, places, passed)]].set(jnp.asarray(lengths, jnp.int32))

    lengths = jnp.where(number % 4 == 0, named(heavy_load, number // 4), named(usual, number - number // 4 - 1))
    mixed = jax.random.permutation(jax.random.fold_in(own, 3), amount)
    donor, sink = mixed[0:amount // 2 * 2:2], mixed[1:amount // 2 * 2:2]
    slack = jnp.minimum(lengths[donor] - 1, bound - lengths[sink]) // 2
    slack = jnp.where((donor == sequence[0]) | (sink == sequence[0]) | (lengths[sink] == 0), 0, jnp.maximum(slack, 0))
    passed = jax.random.randint(jax.random.fold_in(own, 4), (amount // 2,), 0, 1 << 20) % (slack + 1)
    lengths = lengths.at[donor].add(-passed).at[sink].add(passed)
    items = jnp.searchsorted(jnp.cumsum(lengths), jnp.arange(rows * top), side="right").astype(jnp.int32)
    grid = items.reshape(top, rows).T
    grid = grid[jax.random.permutation(jax.random.fold_in(own, 1), rows)]
    offset_by = jax.random.randint(jax.random.fold_in(own, 2), (rows, 1), 0, top)
    return jnp.take_along_axis(grid, (jnp.arange(top)[None, :] + offset_by) % top, axis=1)


def portions_of(amount, total, limit, skew, full):
    weights = [(1 << 20) // math.isqrt(rank ** skew) + 1 for rank in range(1, amount + 1)]
    largest = limit if full else min(limit, max(-(-total // amount), total * weights[0] // sum(weights)))
    least = 1 if total - largest >= amount - 1 else 0
    counts, surplus = [largest] + [least] * (amount - 1), total - largest - least * (amount - 1)
    while surplus > 0:
        candidates = [i for i in range(1, amount) if counts[i] < largest] or [i for i in range(1, amount) if counts[i] < limit]
        mass, left = sum([weights[i] for i in candidates]), surplus
        for i in candidates:
            more = min(limit - counts[i], max(1, left * weights[i] // mass), surplus)
            counts[i] = counts[i] + more
            surplus = surplus - more
    return np.array(counts)


def gaussian(key, extent, width, bound, cuts=(), kind=jnp.bfloat16):
    array = width * jax.random.normal(key, extent, jnp.float32)
    if cuts:
        array = array * shard_levels(key, extent, cuts, -0.22, 0.18)
    return jnp.clip(array, -bound, bound).astype(kind)


def setup_inputs(seed: int = 0) -> dict:
    seeds = jax.random.split(jax.random.key(seed), 10)
    ssd_grad = gaussian(seeds[0], (SEQUENCE_TOKENS, MIXER_HEADS * HEAD_DIM), 1.0, 6.0, ((0, 96), (1, 8)))
    in_proj_b = gaussian(seeds[1], (SEQUENCE_TOKENS, STATE), 0.03, 0.1796875, ((0, 96),))
    in_proj_c = gaussian(seeds[2], (SEQUENCE_TOKENS, STATE), 0.03, 0.1796875, ((0, 96),))
    log_decay = draw_log_decay(jax.random.fold_in(seeds[9], 71), 0)
    expert_grad = gaussian(seeds[4], (SEQUENCE_TOKENS, D), 1.0, 6.0, ((0, 768),))
    route_keys = jax.random.split(jax.random.fold_in(seeds[5], 1), SEQUENCE_TOKENS // TOK_DEV)
    route_turns = jax.random.permutation(jax.random.fold_in(seeds[5], 3), SEQUENCE_TOKENS // TOK_DEV)
    route = jax.vmap(lambda own, number: shared_out(jax.random.fold_in(seeds[5], 2), own, number, TOK_DEV, N_EXP, 1, CAP, 2))(route_keys, route_turns).reshape((SEQUENCE_TOKENS, 1))
    gate_prob = jnp.clip(0.1 + 0.9 * jax.random.uniform(seeds[6], (SEQUENCE_TOKENS,), jnp.float32) ** shard_levels(seeds[6], (SEQUENCE_TOKENS,), ((0, 768),), -0.2, 0.2), 0.1, 1.0)
    down_weight = gaussian(seeds[7], (N_EXP, FF, D), FF ** -0.5, 0.21875, ((0, 8),))
    saved_pre = gaussian(seeds[8], (N_CTX, N_EXP, N_EXP, CAP, 2 * FF), 1.0, 6.0, ((0, 96), (1, 8)))
    return {"ssd_grad": ssd_grad, "in_proj_b": in_proj_b, "in_proj_c": in_proj_c, "log_decay": log_decay, "expert_grad": expert_grad, "route": route, "gate_prob": gate_prob, "down_weight": down_weight, "saved_pre": saved_pre}


def block_state(step_input):
    cotangent, c_block, log_steps = step_input
    cumulative = jnp.cumsum(log_steps, axis=1)
    weighted_c = (jnp.exp(cumulative)[:, :, None] * c_block[None].astype(jnp.float32)).astype(jnp.bfloat16)
    local_state = jnp.einsum('htn,thp->hnp', weighted_c.astype(jnp.float32), cotangent.astype(jnp.float32), precision=lax.Precision.HIGHEST)
    return (local_state, jnp.exp(cumulative[:, -1]))

def back_step(state_grad, step_input):
    updated = step_input[0] + step_input[1][:, None, None] * state_grad
    return (updated, state_grad.astype(jnp.bfloat16))

def block_grad(step_input):
    cotangent, b_block, c_block, log_steps, carried = step_input
    cumulative = jnp.cumsum(log_steps, axis=1)
    scores = jnp.dot(c_block, b_block.T, preferred_element_type=jnp.float32)
    log_gap = cumulative[:, :, None] - cumulative[:, None, :]
    causal = jnp.arange(BLOCK, dtype=jnp.int32)[:, None] >= jnp.arange(BLOCK, dtype=jnp.int32)[None, :]
    weights = jnp.where(causal[None], scores[None] * jnp.exp(jnp.minimum(log_gap, 0.0)), 0.0).astype(jnp.bfloat16)
    within_term = jnp.einsum('hts,thp->shp', weights.astype(jnp.float32), cotangent.astype(jnp.float32), precision=lax.Precision.HIGHEST)
    projected = jnp.einsum('sn,hnp->shp', b_block.astype(jnp.float32), carried.astype(jnp.float32), precision=lax.Precision.HIGHEST)
    end_weight = jnp.exp(cumulative[:, -1:] - cumulative).T
    return (within_term + projected * end_weight[:, :, None]).astype(jnp.bfloat16)

def block_send(grad_rows, slot_ids, gate_probs):
    onehot = (slot_ids[:, None] == jnp.arange(N_EXP, dtype=jnp.int32)[None, :]).astype(jnp.int32)
    before = jnp.cumsum(onehot, axis=0, dtype=jnp.int32) - onehot
    slot_rank = lax.optimization_barrier(jnp.sum(before * onehot, axis=1, dtype=jnp.int32))
    slot_index = slot_ids * CAP + slot_rank
    placement = (slot_index[:, None] == jnp.arange(N_EXP * CAP, dtype=jnp.int32)[None, :]).astype(jnp.bfloat16)
    scaled = (gate_probs[:, None] * grad_rows.astype(jnp.float32)).astype(jnp.bfloat16)
    dispatched = jnp.dot(placement.T, scaled, preferred_element_type=jnp.float32).astype(jnp.bfloat16)
    return dispatched.reshape(N_EXP, CAP, D)

def reference(ssd_grad, in_proj_b, in_proj_c, log_decay, expert_grad, route, gate_prob, down_weight, saved_pre):
    blocks = SEQUENCE_TOKENS // BLOCK
    cotangent = ssd_grad.reshape(blocks, BLOCK, MIXER_HEADS, HEAD_DIM)
    b_blocks = in_proj_b.reshape(blocks, BLOCK, STATE)
    c_blocks = in_proj_c.reshape(blocks, BLOCK, STATE)
    log_blocks = log_decay.reshape(MIXER_HEADS, blocks, BLOCK).transpose(1, 0, 2)
    local_state, block_decay = lax.map(block_state, (cotangent, c_blocks, log_blocks))
    start = jnp.zeros((MIXER_HEADS, STATE, HEAD_DIM), jnp.float32)
    ignored, carried = lax.scan(back_step, start, (local_state, block_decay), reverse=True)
    input_grad = lax.map(block_grad, (cotangent, b_blocks, c_blocks, log_blocks, carried))
    input_grad = input_grad.reshape(SEQUENCE_TOKENS, MIXER_HEADS * HEAD_DIM)
    grad_rows = expert_grad.reshape(N_CTX, N_EXP, TOK_DEV, D)
    slot_ids = route.reshape(N_CTX, N_EXP, TOK_DEV)
    gate_probs = gate_prob.reshape(N_CTX, N_EXP, TOK_DEV)
    weight_f32 = down_weight.astype(jnp.float32)

    def group_grad(step_input):
        rows_here, slots_here, probs_here, saved_acts = step_input
        dispatched = jax.vmap(block_send)(rows_here, slots_here, probs_here).transpose(1, 0, 2, 3)
        hidden_grad = jnp.einsum('escd,efd->escf', dispatched.astype(jnp.float32), weight_f32, precision=lax.Precision.HIGHEST)
        saved_f32 = saved_acts.astype(jnp.float32)
        gate_pre = saved_f32[..., :FF]
        up_pre = saved_f32[..., FF:]
        sigmoid_gate = jax.nn.sigmoid(gate_pre)
        gate_part = hidden_grad * up_pre * sigmoid_gate * (1.0 + gate_pre * (1.0 - sigmoid_gate))
        up_part = hidden_grad * gate_pre * sigmoid_gate
        return jnp.concatenate([gate_part, up_part], axis=-1).astype(jnp.bfloat16)
    pre_grad = lax.map(group_grad, (grad_rows, slot_ids, gate_probs, saved_pre))
    return (input_grad, pre_grad)
```

```python
import functools
import math

import jax
import jax.numpy as jnp
from jax import lax
from jax.experimental import pallas as pl
from jax.experimental.pallas import tpu as pltpu
from jax.sharding import PartitionSpec as P

MESH = pl.DeviceIdType.MESH
F32, BF16 = jnp.float32, jnp.bfloat16
BLOCK = 256
PLANE = 8
CHUNKS = 8
LOG2E = math.log2(math.e)
EXTRA = 8
NT = (((1,), (1,)), ((), ()))


def mm(a, b):
    return jnp.dot(a, b, preferred_element_type=F32)


def mm_nt(a, b, precision=None):
    return lax.dot_general(a, b, NT, preferred_element_type=F32, precision=precision)


def iota(shape, dim):
    return lax.broadcasted_iota(jnp.int32, shape, dim)


def decay_rows(d):
    return jnp.broadcast_to(d, (EXTRA, d.shape[1]))


def kernel(
    sizes,
    g_hbm, b_hbm, c_hbm, ld_hbm, x_hbm, route_hbm, gate_hbm, w_hbm, saved_hbm,
    ig_hbm, pg_hbm,
    g, b, c, ld, x, route, gate, w, saved,
    snd, rcv, st1, ph1, st2, ph2, st3, ph3,
    cum, cumt, ls, within, endw, hid, fac_g, fac_u, ig, pg,
    load_sem, out_sem, ss, rs, ss1, rs1, ss2, rs2, ss3, rs3,
):
    n_exp, n_z, heads, width, blocks, cap, ff = sizes
    state = b.shape[1]
    ctx, y = lax.axis_index("ctx"), lax.axis_index("exp")
    z, p = ctx // PLANE, lax.rem(ctx, PLANE)

    def load(i, src, dst):
        copy = pltpu.make_async_copy(src, dst, load_sem.at[i])
        copy.start()
        return copy

    l_route = load(0, route_hbm, route)
    l_gate = load(1, gate_hbm, gate)
    l_x = load(2, x_hbm, x)

    barrier = pltpu.get_barrier_semaphore()

    def greet(device):
        pl.semaphore_signal(barrier, inc=1, device_id=device, device_id_type=MESH)

    for d in (4, 3, 5, 2, 6, 1, 7):
        greet((ctx, lax.rem(y + d, n_exp)))

    def greet_higher(at, carry):
        greet((at * PLANE + p, y))
        return carry

    lax.fori_loop(z + 1, n_z, greet_higher, 0)
    for d in range(1, PLANE):
        greet((z * PLANE + lax.rem(p + d, PLANE), y))

    l_ld = load(3, ld_hbm, ld)
    l_c = load(4, c_hbm, c)
    l_g = load(5, g_hbm, g)
    l_b = load(6, b_hbm, b)
    l_w = load(7, w_hbm, w)
    l_saved = load(8, saved_hbm, saved)

    rows = x.shape[0]
    slots = n_exp * cap
    l_route.wait()
    l_gate.wait()
    which = route[...]
    onehot = jnp.where(iota((n_exp, rows), 0) == which, 1.0, 0.0)
    earlier = jnp.where(iota((rows, rows), 0) < iota((rows, rows), 1), 1.0, 0.0).astype(BF16)
    before = mm(onehot.astype(BF16), earlier)
    rank = jnp.sum(before * onehot, axis=0, keepdims=True)
    slot = which * cap + rank.astype(jnp.int32)
    here = iota((slots, rows), 0) == slot
    slot_gate = jnp.sum(jnp.where(here, gate[...], 0.0), axis=1, keepdims=True)
    pick = jnp.where(here, 1.0, 0.0).astype(BF16)
    chunk = x.shape[1] // CHUNKS
    half = chunk // 2
    l_x.wait()

    def pack(i):
        part = mm(pick, x[:, i * chunk:(i + 1) * chunk]) * slot_gate
        for e in range(n_exp):
            mine = part[e * cap:(e + 1) * cap]
            both = jnp.concatenate([mine[:, :half], mine[:, half:]], axis=0)
            snd[i, e] = both.astype(BF16)

    for i in range(CHUNKS):
        pack(i)

    pl.semaphore_wait(barrier, n_exp - 1 + PLANE - 1 + z)

    def row_copy(i, d):
        to = lax.rem(y + d, n_exp)
        return pltpu.make_async_remote_copy(
            src_ref=snd.at[i, to], dst_ref=rcv.at[i, y],
            send_sem=ss.at[i, d], recv_sem=rs.at[i, d],
            device_id=(ctx, to), device_id_type=MESH,
        )

    for i in range(CHUNKS):
        for d in (4, 3, 5, 2, 6, 1, 7):
            row_copy(i, d).start()

    l_ld.wait()
    up = jnp.where(iota((BLOCK, BLOCK), 0) <= iota((BLOCK, BLOCK), 1), 1.0, 0.0)
    down = jnp.where(iota((BLOCK, BLOCK), 1) <= iota((BLOCK, BLOCK), 0), 1.0, 0.0)
    for k in range(blocks):
        steps = ld[:, k * BLOCK:(k + 1) * BLOCK]
        cum[k] = jnp.dot(steps, up, preferred_element_type=F32, precision=lax.Precision.HIGHEST)
        cumt[k] = mm_nt(down, steps, precision=lax.Precision.HIGHEST)

    columns = heads * width
    own_lane = iota((heads, columns), 1) // width == iota((heads, columns), 0)

    def spread(column):
        wide = jnp.where(own_lane, jnp.broadcast_to(column, (heads, columns)), 0.0)
        return jnp.sum(wide, axis=0, keepdims=True)

    decay = [jnp.exp(cum[k][:, BLOCK - 1:BLOCK]) for k in range(blocks)]
    decay_row = [spread(d) for d in decay]

    group = 256
    per = group // width
    lane_head = iota((BLOCK, group), 1) // width

    def own_columns(part):
        return jnp.concatenate(
            [jnp.where(lane_head == j, part, jnp.zeros_like(part)) for j in range(per)], axis=0
        )

    l_c.wait()
    l_g.wait()
    eye = jnp.where(iota((state, state), 0) == iota((state, state), 1), 1.0, 0.0).astype(BF16)

    def local(k, carry):
        at = pl.multiple_of(k * BLOCK, BLOCK)
        ct = mm_nt(eye, c[pl.ds(at, BLOCK), :])
        grown = jnp.exp(cum[k])
        for q in range(heads // per):
            left = jnp.concatenate(
                [(ct * grown[q * per + j:q * per + j + 1, :]).astype(BF16) for j in range(per)],
                axis=1,
            )
            right = own_columns(g[pl.ds(at, BLOCK), q * group:(q + 1) * group])
            ls[k, :, q * group:(q + 1) * group] = mm(left, right)
        return carry

    lax.fori_loop(0, blocks, local, 0)

    total = ls[blocks - 1]
    for k in reversed(range(blocks - 1)):
        total = ls[k] + decay_row[k] * total
    whole_decay = decay[0]
    for k in range(1, blocks):
        whole_decay = whole_decay * decay[k]
    total_t = total.T
    wide_decay = jnp.broadcast_to(whole_decay, (heads, state))
    for h in range(heads):
        st1[h, :width, :] = total_t[h * width:(h + 1) * width, :]
        st1[h, width:, :] = decay_rows(wide_decay[h:h + 1, :])

    def plane_copy(src, dst, s_sem, r_sem, d):
        to = lax.rem(p + d, PLANE)
        return pltpu.make_async_remote_copy(
            src_ref=src.at[to], dst_ref=dst.at[p],
            send_sem=s_sem.at[d], recv_sem=r_sem.at[d],
            device_id=(z * PLANE + to, y), device_id_type=MESH,
        )

    for d in range(1, PLANE):
        plane_copy(st1, ph1, ss1, rs1, d).start()
    ph1[p] = st1[p]

    l_b.wait()
    later = iota((BLOCK, BLOCK), 1) >= iota((BLOCK, BLOCK), 0)

    def inside(k, carry):
        at = pl.multiple_of(k * BLOCK, BLOCK)
        scores = mm_nt(b[pl.ds(at, BLOCK), :], c[pl.ds(at, BLOCK), :])
        scores = jnp.where(later, scores, 0.0)
        across = cum[k] * LOG2E
        along = cumt[k] * LOG2E
        for q in range(heads // per):
            parts = []
            for j in range(per):
                h = q * per + j
                gap = jnp.minimum(across[h:h + 1, :] - along[:, h:h + 1], 0.0)
                parts.append((scores * jnp.exp2(gap)).astype(BF16))
            left = jnp.concatenate(parts, axis=1)
            right = own_columns(g[pl.ds(at, BLOCK), q * group:(q + 1) * group])
            within[pl.ds(at, BLOCK), q * group:(q + 1) * group] = mm(left, right)
        rest = jnp.exp2(along[BLOCK - 1:BLOCK, :] - along)
        first = iota((BLOCK, 2 * width), 1) < width
        for q in range(heads // 2):
            endw[pl.ds(at, BLOCK), q * 2 * width:(q + 1) * 2 * width] = jnp.where(
                first, rest[:, 2 * q:2 * q + 1], rest[:, 2 * q + 1:2 * q + 2]
            )
        return carry

    lax.fori_loop(0, blocks // 2, inside, 0)

    for d in range(1, PLANE):
        plane_copy(st1, ph1, ss1, rs1, d).wait_recv()

    def parts_of(ref, at):
        return (
            ref[at, :width, :],
            ref[at, width:width + 1, :],
        )

    plane_sum, plane_decay = parts_of(ph1, PLANE - 1)
    for i in reversed(range(PLANE - 1)):
        s, d = parts_of(ph1, i)
        plane_sum = s + d * plane_sum
        plane_decay = plane_decay * d
    st2[:width, :] = plane_sum
    st2[width:, :] = decay_rows(plane_decay)

    def z_copy(to, at):
        return pltpu.make_async_remote_copy(
            src_ref=st2, dst_ref=ph2.at[at],
            send_sem=ss2.at[to], recv_sem=rs2.at[at],
            device_id=(to * PLANE + p, y), device_id_type=MESH,
        )

    def send_lower(to, carry):
        z_copy(to, z).start()
        return carry

    lax.fori_loop(0, z, send_lower, 0)

    lax.fori_loop(blocks // 2, blocks, inside, 0)

    l_saved.wait()

    def factors(s, carry):
        pre = saved[s].astype(F32)
        gate_pre, up_pre = pre[:, :ff], pre[:, ff:]
        sig = 1.0 / (1.0 + jnp.exp(-gate_pre))
        fac_g[s] = up_pre * sig * (1.0 + gate_pre * (1.0 - sig))
        fac_u[s] = gate_pre * sig
        return carry

    lax.fori_loop(0, n_exp, factors, 0)

    l_w.wait()

    def expert(i):
        rcv[i, y] = snd[i, y]
        for d in range(1, n_exp):
            row_copy(i, d).wait_recv()
        got = [rcv[i, s].astype(F32) for s in range(n_exp)]
        left = jnp.concatenate([m[:cap] for m in got], axis=0)
        right = jnp.concatenate([m[cap:] for m in got], axis=0)
        arrived = jnp.concatenate([left, right], axis=1).astype(BF16)
        part = mm_nt(arrived, w[:, i * chunk:(i + 1) * chunk])
        if i == 0:
            hid[...] = part
        elif i < CHUNKS - 1:
            hid[...] += part
        else:
            part = hid[...] + part
            for s in range(n_exp):
                mine = part[s * cap:(s + 1) * cap]
                pg[s, :, :ff] = (mine * fac_g[s]).astype(BF16)
                pg[s, :, ff:] = (mine * fac_u[s]).astype(BF16)

    expert(0)
    expert(1)

    def from_higher(j, incoming):
        at = n_z - 1 - j
        z_copy(0, at).wait_recv()
        s, d = parts_of(ph2, at)
        return s + d * incoming

    incoming = lax.fori_loop(0, n_z - 1 - z, from_higher, jnp.zeros((width, state), F32))
    for i in reversed(range(PLANE)):
        st3[i] = incoming
        if i > 0:
            s, d = parts_of(ph1, i)
            incoming = s + d * incoming
    for d in range(1, PLANE):
        plane_copy(st3, ph3, ss3, rs3, d).start()
    ph3[p] = st3[p]

    expert(2)
    expert(3)

    for d in range(1, PLANE):
        plane_copy(st3, ph3, ss3, rs3, d).wait_recv()
    carried = jnp.concatenate([ph3[h] for h in range(heads)], axis=0).T
    stores = []
    for k in reversed(range(blocks)):
        here = slice(k * BLOCK, (k + 1) * BLOCK)
        projected = mm(b[here, :], carried.astype(BF16))
        ig[here, :] = (within[here, :] + projected * endw[here, :]).astype(BF16)
        store = pltpu.make_async_copy(ig.at[here], ig_hbm.at[here], out_sem.at[k])
        store.start()
        stores.append(store)
        if k > 0:
            carried = ls[k] + decay_row[k] * carried

    for i in range(4, CHUNKS):
        expert(i)
    store = pltpu.make_async_copy(pg, pg_hbm, out_sem.at[blocks])
    store.start()
    stores.append(store)

    for i in range(CHUNKS):
        for d in range(1, n_exp):
            row_copy(i, d).wait_send()
    for d in range(1, PLANE):
        plane_copy(st1, ph1, ss1, rs1, d).wait_send()
        plane_copy(st3, ph3, ss3, rs3, d).wait_send()

    def sent_lower(to, carry):
        z_copy(to, z).wait_send()
        return carry

    lax.fori_loop(0, z, sent_lower, 0)
    for store in stores:
        store.wait()


def body(
    ssd_grad, in_proj_b, in_proj_c, log_decay, expert_grad, route, gate_prob, down_weight, saved_pre
):
    n_exp, n_z = lax.axis_size("exp"), lax.axis_size("ctx") // PLANE
    rows_seq, columns = ssd_grad.shape
    heads = log_decay.shape[0]
    width = columns // heads
    blocks = rows_seq // BLOCK
    state = in_proj_b.shape[1]
    rows, d_model = expert_grad.shape
    cap, ff = saved_pre.shape[3], down_weight.shape[1]
    half = d_model // CHUNKS // 2
    sizes = (n_exp, n_z, heads, width, blocks, cap, ff)
    dma = pltpu.SemaphoreType.DMA
    vmem = pltpu.VMEM
    scratch = [
        vmem((rows_seq, columns), BF16), vmem((rows_seq, state), BF16), vmem((rows_seq, state), BF16),
        vmem((heads, rows_seq), F32), vmem((rows, d_model), BF16), vmem((1, rows), jnp.int32),
        vmem((1, rows), F32), vmem((ff, d_model), BF16), vmem((n_exp, cap, 2 * ff), BF16),
        vmem((CHUNKS, n_exp, 2 * cap, half), BF16), vmem((CHUNKS, n_exp, 2 * cap, half), BF16),
        vmem((PLANE, width + EXTRA, state), F32), vmem((PLANE, width + EXTRA, state), F32),
        vmem((width + EXTRA, state), F32), vmem((n_z, width + EXTRA, state), F32),
        vmem((PLANE, width, state), F32), vmem((PLANE, width, state), F32),
        vmem((blocks, heads, BLOCK), F32), vmem((blocks, BLOCK, heads), F32),
        vmem((blocks, state, columns), F32), vmem((rows_seq, columns), F32),
        vmem((rows_seq, columns), F32), vmem((n_exp * cap, ff), F32),
        vmem((n_exp, cap, ff), F32), vmem((n_exp, cap, ff), F32),
        vmem((rows_seq, columns), BF16), vmem((n_exp, cap, 2 * ff), BF16),
        dma((9,)), dma((blocks + 1,)), dma((CHUNKS, n_exp)), dma((CHUNKS, n_exp)),
        dma((PLANE,)), dma((PLANE,)), dma((n_z,)), dma((n_z,)), dma((PLANE,)), dma((PLANE,)),
    ]
    any_space = pl.BlockSpec(memory_space=pl.ANY)
    input_grad, pre_grad = pl.pallas_call(
        functools.partial(kernel, sizes),
        out_shape=(
            jax.ShapeDtypeStruct((rows_seq, columns), BF16),
            jax.ShapeDtypeStruct((n_exp, cap, 2 * ff), BF16),
        ),
        in_specs=[any_space] * 9,
        out_specs=(any_space, any_space),
        scratch_shapes=scratch,
        compiler_params=pltpu.CompilerParams(
            collective_id=0, has_side_effects=True, vmem_limit_bytes=56 * 2**20
        ),
        name="hybrid",
    )(
        ssd_grad, in_proj_b, in_proj_c, log_decay, expert_grad,
        route.reshape(1, rows), gate_prob.reshape(1, rows), down_weight[0], saved_pre[0, 0],
    )
    return input_grad, pre_grad[None, None]


def solution(mesh):
    placed = (
        P("ctx", "exp"),
        P("ctx", None),
        P("ctx", None),
        P("exp", "ctx"),
        P(("ctx", "exp"), None),
        P(("ctx", "exp"), None),
        P(("ctx", "exp")),
        P("exp", None, None),
        P("ctx", "exp", None, None, None),
    )
    return jax.shard_map(
        body,
        mesh=mesh,
        in_specs=placed,
        out_specs=(P("ctx", "exp"), P("ctx", "exp", None, None, None)),
        check_vma=False,
    )
```

```python
import functools
import math

import jax
import jax.numpy as jnp
from jax import lax
from jax.experimental import pallas as pl
from jax.experimental.pallas import tpu as pltpu
from jax.sharding import PartitionSpec as P

MESH = pl.DeviceIdType.MESH
F32, BF16, I16 = jnp.float32, jnp.bfloat16, jnp.int16
BLOCK = 256
PLANE = 8
Z_GROUP = 3
CHUNKS = 4
LOG2E = math.log2(math.e)
EXTRA, EXTRA16, ONE16 = 8, 16, 14
NT = (((1,), (1,)), ((), ()))


def mm(a, b):
    return jnp.dot(a, b, preferred_element_type=F32)


def mm_nt(a, b, precision=None):
    return lax.dot_general(a, b, NT, preferred_element_type=F32, precision=precision)


def iota(shape, dim):
    return lax.broadcasted_iota(jnp.int32, shape, dim)


def decay_rows(d):
    return jnp.broadcast_to(d, (EXTRA, d.shape[1]))


def to_fixed(value, d):
    top = jnp.max(jnp.abs(value), axis=(0, 1), keepdims=True)
    power = jnp.ceil(jnp.log2(jnp.maximum(top, 1e-30)))
    power = jnp.broadcast_to(power, (1, value.shape[1]))
    coded = jnp.round(value * jnp.exp2(ONE16 - power))
    high = jnp.floor(d * 2.0**ONE16)
    low = jnp.round((d * 2.0**ONE16 - high) * 2.0**ONE16)
    row = iota((EXTRA16, value.shape[1]), 0)
    rows = jnp.where(row == 0, power, jnp.where(row == 1, high, low))
    return jnp.concatenate([coded, rows], axis=0).astype(jnp.int32).astype(jnp.int16)


def from_fixed(coded, width):
    wide = coded.astype(jnp.int32).astype(F32)
    rows = wide[width:width + 8]
    value = wide[:width] * jnp.exp2(rows[0:1] - ONE16)
    return value, (rows[1:2] + rows[2:3] * 2.0**-ONE16) * 2.0**-ONE16


def kernel(
    sizes,
    g_hbm, b_hbm, c_hbm, ld_hbm, x_hbm, route_hbm, gate_hbm, w_hbm, saved_hbm,
    ig_hbm, pg_hbm,
    g, b, c, ld, x, route, gate, w, saved,
    snd, rcv, st1, ph1, st2, ph2, st3, ph3, st4, ph4,
    cum, cumt, ls, within, endw, hid, fac_g, fac_u, ig, pg,
    load_sem, out_sem, ss, rs, ss1, rs1, ss2, rs2, ss3, rs3, ss4, rs4,
):
    n_exp, n_z, heads, width, blocks, cap, ff = sizes
    state = b.shape[1]
    ctx, y = lax.axis_index("ctx"), lax.axis_index("exp")
    z, p = ctx // PLANE, lax.rem(ctx, PLANE)

    def load(i, src, dst):
        copy = pltpu.make_async_copy(src, dst, load_sem.at[i])
        copy.start()
        return copy

    l_route = load(0, route_hbm, route)
    l_gate = load(1, gate_hbm, gate)
    l_x = load(2, x_hbm, x)

    barrier = pltpu.get_barrier_semaphore()

    def greet(device):
        pl.semaphore_signal(barrier, inc=1, device_id=device, device_id_type=MESH)

    for d in (4, 3, 5, 2, 6, 1, 7):
        greet((ctx, lax.rem(y + d, n_exp)))

    in_group = lax.rem(z, Z_GROUP)
    first = z - in_group
    group_at = z // Z_GROUP
    group_end = jnp.minimum(first + Z_GROUP, n_z)
    groups = -(-n_z // Z_GROUP)

    def greet_plane(at, carry):
        greet((at * PLANE + p, y))
        return carry

    def greet_group(at, carry):
        greet((at * Z_GROUP * PLANE + p, y))
        return carry

    lax.fori_loop(z + 1, group_end, greet_plane, 0)
    lax.fori_loop(group_at + 1, groups, greet_group, 0)
    for d in range(1, PLANE):
        greet((z * PLANE + lax.rem(p + d, PLANE), y))

    l_ld = load(3, ld_hbm, ld)
    l_c = load(4, c_hbm, c)
    l_g = load(5, g_hbm, g)
    l_b = load(6, b_hbm, b)
    l_w = load(7, w_hbm, w)
    l_saved = load(8, saved_hbm, saved)

    rows = x.shape[0]
    slots = n_exp * cap
    l_route.wait()
    l_gate.wait()
    which = route[...]
    onehot = jnp.where(iota((n_exp, rows), 0) == which, 1.0, 0.0)
    earlier = jnp.where(iota((rows, rows), 0) < iota((rows, rows), 1), 1.0, 0.0).astype(BF16)
    before = mm(onehot.astype(BF16), earlier)
    rank = jnp.sum(before * onehot, axis=0, keepdims=True)
    slot = which * cap + rank.astype(jnp.int32)
    here = iota((slots, rows), 0) == slot
    slot_gate = jnp.sum(jnp.where(here, gate[...], 0.0), axis=1, keepdims=True)
    pick = jnp.where(here, 1.0, 0.0).astype(BF16)
    chunk = x.shape[1] // CHUNKS
    half = chunk // 2
    l_x.wait()

    def pack(i):
        part = mm(pick, x[:, i * chunk:(i + 1) * chunk]) * slot_gate
        for e in range(n_exp):
            mine = part[e * cap:(e + 1) * cap]
            both = jnp.concatenate([mine[:, :half], mine[:, half:]], axis=0)
            snd[i, e] = both.astype(BF16)

    for i in range(CHUNKS):
        pack(i)

    def row_copy(i, d):
        to = lax.rem(y + d, n_exp)
        return pltpu.make_async_remote_copy(
            src_ref=snd.at[i, to], dst_ref=rcv.at[i, y],
            send_sem=ss.at[i, d], recv_sem=rs.at[i, d],
            device_id=(ctx, to), device_id_type=MESH,
        )

    l_ld.wait()
    up = jnp.where(iota((BLOCK, BLOCK), 0) <= iota((BLOCK, BLOCK), 1), 1.0, 0.0)
    down = jnp.where(iota((BLOCK, BLOCK), 1) <= iota((BLOCK, BLOCK), 0), 1.0, 0.0)
    for k in range(blocks):
        steps = ld[:, k * BLOCK:(k + 1) * BLOCK]
        cum[k] = jnp.dot(steps, up, preferred_element_type=F32, precision=lax.Precision.HIGHEST)
        cumt[k] = mm_nt(down, steps, precision=lax.Precision.HIGHEST)

    columns = heads * width
    own_lane = iota((heads, columns), 1) // width == iota((heads, columns), 0)

    def spread(column):
        wide = jnp.where(own_lane, jnp.broadcast_to(column, (heads, columns)), 0.0)
        return jnp.sum(wide, axis=0, keepdims=True)

    decay = [jnp.exp(cum[k][:, BLOCK - 1:BLOCK]) for k in range(blocks)]
    decay_row = [spread(d) for d in decay]

    group = 256
    per = group // width
    lane_head = iota((BLOCK, group), 1) // width

    def own_columns(part):
        return jnp.concatenate(
            [jnp.where(lane_head == j, part, jnp.zeros_like(part)) for j in range(per)], axis=0
        )

    lower = jnp.where(in_group == 0, z, 0)
    pl.semaphore_wait(barrier, n_exp - 1 + PLANE - 1 + in_group + lower)

    for i in range(CHUNKS):
        for d in (4, 3, 5, 2, 6, 1, 7):
            row_copy(i, d).start()

    l_c.wait()
    l_g.wait()
    eye = jnp.where(iota((state, state), 0) == iota((state, state), 1), 1.0, 0.0).astype(BF16)

    def local(k, carry):
        at = pl.multiple_of(k * BLOCK, BLOCK)
        ct = mm_nt(eye, c[pl.ds(at, BLOCK), :])
        grown = jnp.exp(cum[k])
        for q in range(heads // per):
            left = jnp.concatenate(
                [(ct * grown[q * per + j:q * per + j + 1, :]).astype(BF16) for j in range(per)],
                axis=1,
            )
            right = own_columns(g[pl.ds(at, BLOCK), q * group:(q + 1) * group])
            ls[k, :, q * group:(q + 1) * group] = mm(left, right)
        return carry

    lax.fori_loop(0, blocks, local, 0)

    total = ls[blocks - 1]
    for k in reversed(range(blocks - 1)):
        inner = total
        total = ls[k] + decay_row[k] * inner
        ls[k] = inner
    whole_decay = decay[0]
    for k in range(1, blocks):
        whole_decay = whole_decay * decay[k]
    total_t = total.T
    wide_decay = jnp.broadcast_to(whole_decay, (heads, state))
    for h in range(heads):
        st1[h, :width, :] = total_t[h * width:(h + 1) * width, :]
        st1[h, width:, :] = decay_rows(wide_decay[h:h + 1, :])

    def plane_copy(src, dst, s_sem, r_sem, d):
        to = lax.rem(p + d, PLANE)
        return pltpu.make_async_remote_copy(
            src_ref=src.at[to], dst_ref=dst.at[p],
            send_sem=s_sem.at[d], recv_sem=r_sem.at[d],
            device_id=(z * PLANE + to, y), device_id_type=MESH,
        )

    for d in range(1, PLANE):
        plane_copy(st1, ph1, ss1, rs1, d).start()
    ph1[p] = st1[p]

    l_b.wait()
    later = iota((BLOCK, BLOCK), 1) >= iota((BLOCK, BLOCK), 0)

    def inside(k, carry):
        at = pl.multiple_of(k * BLOCK, BLOCK)
        scores = mm_nt(b[pl.ds(at, BLOCK), :], c[pl.ds(at, BLOCK), :])
        scores = jnp.where(later, scores, 0.0)
        across = cum[k] * LOG2E
        along = cumt[k] * LOG2E
        for q in range(heads // per):
            parts = []
            for j in range(per):
                h = q * per + j
                gap = jnp.minimum(across[h:h + 1, :] - along[:, h:h + 1], 0.0)
                parts.append((scores * jnp.exp2(gap)).astype(BF16))
            left = jnp.concatenate(parts, axis=1)
            right = own_columns(g[pl.ds(at, BLOCK), q * group:(q + 1) * group])
            within[pl.ds(at, BLOCK), q * group:(q + 1) * group] = mm(left, right)
        rest = jnp.exp2(along[BLOCK - 1:BLOCK, :] - along)
        first = iota((BLOCK, 2 * width), 1) < width
        for q in range(heads // 2):
            endw[pl.ds(at, BLOCK), q * 2 * width:(q + 1) * 2 * width] = jnp.where(
                first, rest[:, 2 * q:2 * q + 1], rest[:, 2 * q + 1:2 * q + 2]
            )
        return carry

    lax.fori_loop(0, blocks, inside, 0)

    for d in range(1, PLANE):
        plane_copy(st1, ph1, ss1, rs1, d).wait_recv()

    def parts_of(ref, at):
        return (
            ref[at, :width, :],
            ref[at, width:width + 1, :],
        )

    plane_sum, plane_decay = parts_of(ph1, PLANE - 1)
    for i in reversed(range(PLANE - 1)):
        s, d = parts_of(ph1, i)
        plane_sum = s + d * plane_sum
        plane_decay = plane_decay * d
    st2[:width, :] = plane_sum
    st2[width:, :] = decay_rows(plane_decay)

    def z_copy(to, at):
        return pltpu.make_async_remote_copy(
            src_ref=st2, dst_ref=ph2.at[at],
            send_sem=ss2.at[to], recv_sem=rs2.at[at],
            device_id=(to * PLANE + p, y), device_id_type=MESH,
        )

    def group_copy(to, at):
        return pltpu.make_async_remote_copy(
            src_ref=st4, dst_ref=ph4.at[at],
            send_sem=ss4.at[to], recv_sem=rs4.at[at],
            device_id=(to * PLANE + p, y), device_id_type=MESH,
        )

    def send_plane(to, carry):
        z_copy(to, z).start()
        return carry

    def send_group(to, carry):
        group_copy(to, group_at).start()
        return carry

    lax.fori_loop(first, z, send_plane, 0)

    def from_plane(at, carry):
        incoming, reach = carry
        z_copy(0, at).wait_recv()
        s, d = parts_of(ph2, at)
        return incoming + reach * s, reach * d

    none = (jnp.zeros((width, state), F32), jnp.ones((1, state), F32))
    later_planes = lax.fori_loop(z + 1, group_end, from_plane, none)

    @pl.when(in_group == 0)
    def _():
        st4[...] = to_fixed(
            plane_sum + plane_decay * later_planes[0], plane_decay * later_planes[1]
        )
        lax.fori_loop(0, first, send_group, 0)

    l_saved.wait()

    def factors(s, carry):
        pre = saved[s].astype(F32)
        gate_pre, up_pre = pre[:, :ff], pre[:, ff:]
        sig = 1.0 / (1.0 + jnp.exp(-gate_pre))
        fac_g[s] = up_pre * sig * (1.0 + gate_pre * (1.0 - sig))
        fac_u[s] = gate_pre * sig
        return carry

    lax.fori_loop(0, n_exp, factors, 0)

    l_w.wait()

    def expert(i):
        rcv[i, y] = snd[i, y]
        for d in range(1, n_exp):
            row_copy(i, d).wait_recv()
        got = [rcv[i, s].astype(F32) for s in range(n_exp)]
        left = jnp.concatenate([m[:cap] for m in got], axis=0)
        right = jnp.concatenate([m[cap:] for m in got], axis=0)
        arrived = jnp.concatenate([left, right], axis=1).astype(BF16)
        part = mm_nt(arrived, w[:, i * chunk:(i + 1) * chunk])
        if i == 0:
            hid[...] = part
        elif i < CHUNKS - 1:
            hid[...] += part
        else:
            part = hid[...] + part
            for s in range(n_exp):
                mine = part[s * cap:(s + 1) * cap]
                pg[s, :, :ff] = (mine * fac_g[s]).astype(BF16)
                pg[s, :, ff:] = (mine * fac_u[s]).astype(BF16)

    def from_group(at, carry):
        incoming, reach = carry
        group_copy(0, at).wait_recv()
        s, d = from_fixed(ph4[at], width)
        return incoming + reach * s, reach * d

    incoming = lax.fori_loop(group_at + 1, groups, from_group, later_planes)[0]
    for i in reversed(range(PLANE)):
        st3[i] = incoming
        if i > 0:
            s, d = parts_of(ph1, i)
            incoming = s + d * incoming
    for d in range(1, PLANE):
        plane_copy(st3, ph3, ss3, rs3, d).start()
    ph3[p] = st3[p]

    expert(0)

    for d in range(1, PLANE):
        plane_copy(st3, ph3, ss3, rs3, d).wait_recv()
    incoming = jnp.concatenate([ph3[h] for h in range(heads)], axis=0).T
    stores = []
    reach = None
    for k in reversed(range(blocks)):
        here = slice(k * BLOCK, (k + 1) * BLOCK)
        if reach is None:
            carried = incoming
        else:
            carried = ls[k] + reach * incoming
        reach = decay_row[k] if reach is None else reach * decay_row[k]
        projected = mm(b[here, :], carried.astype(BF16))
        ig[here, :] = (within[here, :] + projected * endw[here, :]).astype(BF16)
        store = pltpu.make_async_copy(ig.at[here], ig_hbm.at[here], out_sem.at[k])
        store.start()
        stores.append(store)

    for i in range(1, CHUNKS):
        expert(i)
    store = pltpu.make_async_copy(pg, pg_hbm, out_sem.at[blocks])
    store.start()
    stores.append(store)

    for i in range(CHUNKS):
        for d in range(1, n_exp):
            row_copy(i, d).wait_send()
    for d in range(1, PLANE):
        plane_copy(st1, ph1, ss1, rs1, d).wait_send()
        plane_copy(st3, ph3, ss3, rs3, d).wait_send()

    def sent_plane(to, carry):
        z_copy(to, z).wait_send()
        return carry

    def sent_group(to, carry):
        group_copy(to, group_at).wait_send()
        return carry

    lax.fori_loop(first, z, sent_plane, 0)
    lax.fori_loop(0, lower, sent_group, 0)
    for store in stores:
        store.wait()


def body(
    ssd_grad, in_proj_b, in_proj_c, log_decay, expert_grad, route, gate_prob, down_weight, saved_pre
):
    n_exp, n_z = lax.axis_size("exp"), lax.axis_size("ctx") // PLANE
    rows_seq, columns = ssd_grad.shape
    heads = log_decay.shape[0]
    width = columns // heads
    blocks = rows_seq // BLOCK
    state = in_proj_b.shape[1]
    rows, d_model = expert_grad.shape
    cap, ff = saved_pre.shape[3], down_weight.shape[1]
    half = d_model // CHUNKS // 2
    sizes = (n_exp, n_z, heads, width, blocks, cap, ff)
    dma = pltpu.SemaphoreType.DMA
    vmem = pltpu.VMEM
    scratch = [
        vmem((rows_seq, columns), BF16), vmem((rows_seq, state), BF16), vmem((rows_seq, state), BF16),
        vmem((heads, rows_seq), F32), vmem((rows, d_model), BF16), vmem((1, rows), jnp.int32),
        vmem((1, rows), F32), vmem((ff, d_model), BF16), vmem((n_exp, cap, 2 * ff), BF16),
        vmem((CHUNKS, n_exp, 2 * cap, half), BF16), vmem((CHUNKS, n_exp, 2 * cap, half), BF16),
        vmem((PLANE, width + EXTRA, state), F32), vmem((PLANE, width + EXTRA, state), F32),
        vmem((width + EXTRA, state), F32), vmem((n_z, width + EXTRA, state), F32),
        vmem((PLANE, width, state), F32), vmem((PLANE, width, state), F32),
        vmem((width + EXTRA16, state), I16), vmem((n_z, width + EXTRA16, state), I16),
        vmem((blocks, heads, BLOCK), F32), vmem((blocks, BLOCK, heads), F32),
        vmem((blocks, state, columns), F32), vmem((rows_seq, columns), F32),
        vmem((rows_seq, columns), F32), vmem((n_exp * cap, ff), F32),
        vmem((n_exp, cap, ff), F32), vmem((n_exp, cap, ff), F32),
        vmem((rows_seq, columns), BF16), vmem((n_exp, cap, 2 * ff), BF16),
        dma((9,)), dma((blocks + 1,)), dma((CHUNKS, n_exp)), dma((CHUNKS, n_exp)),
        dma((PLANE,)), dma((PLANE,)), dma((n_z,)), dma((n_z,)), dma((PLANE,)), dma((PLANE,)),
        dma((n_z,)), dma((n_z,)),
    ]
    any_space = pl.BlockSpec(memory_space=pl.ANY)
    input_grad, pre_grad = pl.pallas_call(
        functools.partial(kernel, sizes),
        out_shape=(
            jax.ShapeDtypeStruct((rows_seq, columns), BF16),
            jax.ShapeDtypeStruct((n_exp, cap, 2 * ff), BF16),
        ),
        in_specs=[pl.BlockSpec(memory_space=pltpu.HBM)] * 9,
        out_specs=(any_space, any_space),
        scratch_shapes=scratch,
        compiler_params=pltpu.CompilerParams(
            collective_id=0, has_side_effects=True, vmem_limit_bytes=40 * 2**20
        ),
        name="hybrid",
    )(
        *[
            pltpu.with_memory_space_constraint(operand, pltpu.HBM)
            for operand in (
                ssd_grad, in_proj_b, in_proj_c, log_decay, expert_grad, route.reshape(1, rows),
                gate_prob.reshape(1, rows), down_weight[0], saved_pre[0, 0],
            )
        ]
    )
    return input_grad, pre_grad[None, None]


def solution(mesh):
    placed = (
        P("ctx", "exp"),
        P("ctx", None),
        P("ctx", None),
        P("exp", "ctx"),
        P(("ctx", "exp"), None),
        P(("ctx", "exp"), None),
        P(("ctx", "exp")),
        P("exp", None, None),
        P("ctx", "exp", None, None, None),
    )
    return jax.shard_map(
        body,
        mesh=mesh,
        in_specs=placed,
        out_specs=(P("ctx", "exp"), P("ctx", "exp", None, None, None)),
        check_vma=False,
    )
```

```python
import functools
import math

import jax
import jax.numpy as jnp
from jax import lax
from jax.experimental import pallas as pl
from jax.experimental.pallas import tpu as pltpu
from jax.sharding import PartitionSpec as P

MESH = pl.DeviceIdType.MESH
F32, BF16, I16 = jnp.float32, jnp.bfloat16, jnp.int16
BLOCK = 256
PLANE = 8
Z_GROUP = 3
CHUNKS = 4
LOG2E = math.log2(math.e)
EXTRA, EXTRA16, ONE16 = 8, 16, 14
NT = (((1,), (1,)), ((), ()))


def mm(a, b):
    return jnp.dot(a, b, preferred_element_type=F32)


def mm_nt(a, b, precision=None):
    return lax.dot_general(a, b, NT, preferred_element_type=F32, precision=precision)


def iota(shape, dim):
    return lax.broadcasted_iota(jnp.int32, shape, dim)


def decay_rows(d):
    return jnp.broadcast_to(d, (EXTRA, d.shape[1]))


def to_fixed(value, d):
    top = jnp.max(jnp.abs(value), axis=(0, 1), keepdims=True)
    power = jnp.ceil(jnp.log2(jnp.maximum(top, 1e-30)))
    power = jnp.broadcast_to(power, (1, value.shape[1]))
    coded = jnp.round(value * jnp.exp2(ONE16 - power))
    high = jnp.floor(d * 2.0**ONE16)
    low = jnp.round((d * 2.0**ONE16 - high) * 2.0**ONE16)
    row = iota((EXTRA16, value.shape[1]), 0)
    rows = jnp.where(row == 0, power, jnp.where(row == 1, high, low))
    return jnp.concatenate([coded, rows], axis=0).astype(jnp.int32).astype(jnp.int16)


def from_fixed(coded, width):
    wide = coded.astype(jnp.int32).astype(F32)
    rows = wide[width:width + 8]
    value = wide[:width] * jnp.exp2(rows[0:1] - ONE16)
    return value, (rows[1:2] + rows[2:3] * 2.0**-ONE16) * 2.0**-ONE16


def kernel(
    sizes,
    g_hbm, b_hbm, c_hbm, ld_hbm, x_hbm, route_hbm, gate_hbm, w_hbm, saved_hbm,
    ig, pg,
    g, b, c, ld, x, route, gate, w, saved,
    snd, rcv, st1, ph1, st2, ph2, st3, ph3, st4, ph4,
    cum, cumt, ls, within, endw, hid, fac_g, fac_u,
    load_sem, ss, rs, ss1, rs1, ss2, rs2, ss3, rs3, ss4, rs4,
):
    n_exp, n_z, heads, width, blocks, cap, ff = sizes
    state = b.shape[1]
    ctx, y = lax.axis_index("ctx"), lax.axis_index("exp")
    z, p = ctx // PLANE, lax.rem(ctx, PLANE)

    def load(i, src, dst):
        copy = pltpu.make_async_copy(src, dst, load_sem.at[i])
        copy.start()
        return copy

    barrier = pltpu.get_barrier_semaphore()

    def greet(device):
        pl.semaphore_signal(barrier, inc=1, device_id=device, device_id_type=MESH)

    for d in (4, 3, 5, 2, 6, 1, 7):
        greet((ctx, lax.rem(y + d, n_exp)))

    l_route = load(0, route_hbm, route)
    l_gate = load(1, gate_hbm, gate)
    chunk = x.shape[1] // CHUNKS
    half = chunk // 2
    l_x = []
    for i in range(CHUNKS):
        here = slice(i * chunk, (i + 1) * chunk)
        l_x.append(load(9 + i, x_hbm.at[:, here], x.at[:, here]))

    in_group = lax.rem(z, Z_GROUP)
    first = z - in_group
    group_at = z // Z_GROUP
    group_end = jnp.minimum(first + Z_GROUP, n_z)
    groups = -(-n_z // Z_GROUP)

    def greet_plane(at, carry):
        greet((at * PLANE + p, y))
        return carry

    def greet_group(at, carry):
        greet((at * Z_GROUP * PLANE + p, y))
        return carry

    lax.fori_loop(z + 1, group_end, greet_plane, 0)
    lax.fori_loop(group_at + 1, groups, greet_group, 0)
    for d in range(1, PLANE):
        greet((z * PLANE + lax.rem(p + d, PLANE), y))

    l_ld = load(3, ld_hbm, ld)
    l_c = load(4, c_hbm, c)
    l_g = load(5, g_hbm, g)
    l_b = load(6, b_hbm, b)
    l_w = load(7, w_hbm, w)
    l_saved = load(8, saved_hbm, saved)

    rows = x.shape[0]
    slots = n_exp * cap
    l_route.wait()
    l_gate.wait()
    which = route[...]
    onehot = jnp.where(iota((n_exp, rows), 0) == which, 1.0, 0.0)
    earlier = jnp.where(iota((rows, rows), 0) < iota((rows, rows), 1), 1.0, 0.0).astype(BF16)
    before = mm(onehot.astype(BF16), earlier)
    rank = jnp.sum(before * onehot, axis=0, keepdims=True)
    slot = which * cap + rank.astype(jnp.int32)
    here = iota((slots, rows), 0) == slot
    slot_gate = jnp.sum(jnp.where(here, gate[...], 0.0), axis=1, keepdims=True)
    pick = jnp.where(here, 1.0, 0.0).astype(BF16)

    def pack(i):
        l_x[i].wait()
        part = mm(pick, x[:, i * chunk:(i + 1) * chunk]) * slot_gate
        for e in range(n_exp):
            mine = part[e * cap:(e + 1) * cap]
            both = jnp.concatenate([mine[:, :half], mine[:, half:]], axis=0)
            snd[i, e] = both.astype(BF16)

    def row_copy(i, d):
        to = lax.rem(y + d, n_exp)
        return pltpu.make_async_remote_copy(
            src_ref=snd.at[i, to], dst_ref=rcv.at[i, y],
            send_sem=ss.at[i, d], recv_sem=rs.at[i, d],
            device_id=(ctx, to), device_id_type=MESH,
        )

    pack(0)
    l_ld.wait()
    up = jnp.where(iota((BLOCK, BLOCK), 0) <= iota((BLOCK, BLOCK), 1), 1.0, 0.0)
    down = jnp.where(iota((BLOCK, BLOCK), 1) <= iota((BLOCK, BLOCK), 0), 1.0, 0.0)
    for k in range(blocks):
        steps = ld[:, k * BLOCK:(k + 1) * BLOCK]
        cum[k] = jnp.dot(steps, up, preferred_element_type=F32, precision=lax.Precision.HIGHEST)
        cumt[k] = mm_nt(down, steps, precision=lax.Precision.HIGHEST)

    lower = jnp.where(in_group == 0, z, 0)
    pl.semaphore_wait(barrier, n_exp - 1 + PLANE - 1 + in_group + lower)
    for i in range(CHUNKS):
        if i > 0:
            pack(i)
        for d in (4, 3, 5, 2, 6, 1, 7):
            row_copy(i, d).start()

    columns = heads * width
    own_lane = iota((heads, columns), 1) // width == iota((heads, columns), 0)

    def spread(column):
        wide = jnp.where(own_lane, jnp.broadcast_to(column, (heads, columns)), 0.0)
        return jnp.sum(wide, axis=0, keepdims=True)

    decay = [jnp.exp(cum[k][:, BLOCK - 1:BLOCK]) for k in range(blocks)]
    decay_row = [spread(d) for d in decay]

    group = 256
    per = group // width
    lane_head = iota((BLOCK, group), 1) // width

    def own_columns(part):
        return jnp.concatenate(
            [jnp.where(lane_head == j, part, jnp.zeros_like(part)) for j in range(per)], axis=0
        )

    l_c.wait()
    l_g.wait()
    eye = jnp.where(iota((state, state), 0) == iota((state, state), 1), 1.0, 0.0).astype(BF16)

    def local(k, carry):
        at = pl.multiple_of(k * BLOCK, BLOCK)
        ct = mm_nt(eye, c[pl.ds(at, BLOCK), :])
        grown = jnp.exp(cum[k])
        for q in range(heads // per):
            left = jnp.concatenate(
                [(ct * grown[q * per + j:q * per + j + 1, :]).astype(BF16) for j in range(per)],
                axis=1,
            )
            right = own_columns(g[pl.ds(at, BLOCK), q * group:(q + 1) * group])
            ls[k, :, q * group:(q + 1) * group] = mm(left, right)
        return carry

    lax.fori_loop(0, blocks, local, 0)

    total = ls[blocks - 1]
    for k in reversed(range(blocks - 1)):
        inner = total
        total = ls[k] + decay_row[k] * inner
        ls[k] = inner
    whole_decay = decay[0]
    for k in range(1, blocks):
        whole_decay = whole_decay * decay[k]
    total_t = total.T
    wide_decay = jnp.broadcast_to(whole_decay, (heads, state))
    for h in range(heads):
        st1[h, :width, :] = total_t[h * width:(h + 1) * width, :]
        st1[h, width:, :] = decay_rows(wide_decay[h:h + 1, :])

    def plane_copy(src, dst, s_sem, r_sem, d):
        to = lax.rem(p + d, PLANE)
        return pltpu.make_async_remote_copy(
            src_ref=src.at[to], dst_ref=dst.at[p],
            send_sem=s_sem.at[d], recv_sem=r_sem.at[d],
            device_id=(z * PLANE + to, y), device_id_type=MESH,
        )

    for d in range(1, PLANE):
        plane_copy(st1, ph1, ss1, rs1, d).start()
    ph1[p] = st1[p]

    l_b.wait()
    later = iota((BLOCK, BLOCK), 1) >= iota((BLOCK, BLOCK), 0)

    def inside(k, carry):
        at = pl.multiple_of(k * BLOCK, BLOCK)
        scores = mm_nt(b[pl.ds(at, BLOCK), :], c[pl.ds(at, BLOCK), :])
        scores = jnp.where(later, scores, 0.0)
        across = cum[k] * LOG2E
        along = cumt[k] * LOG2E
        for q in range(heads // per):
            parts = []
            for j in range(per):
                h = q * per + j
                gap = jnp.minimum(across[h:h + 1, :] - along[:, h:h + 1], 0.0)
                parts.append((scores * jnp.exp2(gap)).astype(BF16))
            left = jnp.concatenate(parts, axis=1)
            right = own_columns(g[pl.ds(at, BLOCK), q * group:(q + 1) * group])
            within[pl.ds(at, BLOCK), q * group:(q + 1) * group] = mm(left, right)
        rest = jnp.exp2(along[BLOCK - 1:BLOCK, :] - along)
        first = iota((BLOCK, 2 * width), 1) < width
        for q in range(heads // 2):
            endw[pl.ds(at, BLOCK), q * 2 * width:(q + 1) * 2 * width] = jnp.where(
                first, rest[:, 2 * q:2 * q + 1], rest[:, 2 * q + 1:2 * q + 2]
            )
        return carry

    lax.fori_loop(0, blocks, inside, 0)

    for d in range(1, PLANE):
        plane_copy(st1, ph1, ss1, rs1, d).wait_recv()

    def parts_of(ref, at):
        return (
            ref[at, :width, :],
            ref[at, width:width + 1, :],
        )

    plane_sum, plane_decay = parts_of(ph1, PLANE - 1)
    for i in reversed(range(PLANE - 1)):
        s, d = parts_of(ph1, i)
        plane_sum = s + d * plane_sum
        plane_decay = plane_decay * d
    st2[:width, :] = plane_sum
    st2[width:, :] = decay_rows(plane_decay)

    def z_copy(to, at):
        return pltpu.make_async_remote_copy(
            src_ref=st2, dst_ref=ph2.at[at],
            send_sem=ss2.at[to], recv_sem=rs2.at[at],
            device_id=(to * PLANE + p, y), device_id_type=MESH,
        )

    def group_copy(to, at):
        return pltpu.make_async_remote_copy(
            src_ref=st4, dst_ref=ph4.at[at],
            send_sem=ss4.at[to], recv_sem=rs4.at[at],
            device_id=(to * PLANE + p, y), device_id_type=MESH,
        )

    def send_plane(to, carry):
        z_copy(to, z).start()
        return carry

    def send_group(to, carry):
        group_copy(to, group_at).start()
        return carry

    lax.fori_loop(first, z, send_plane, 0)

    def from_plane(at, carry):
        incoming, reach = carry
        z_copy(0, at).wait_recv()
        s, d = parts_of(ph2, at)
        return incoming + reach * s, reach * d

    none = (jnp.zeros((width, state), F32), jnp.ones((1, state), F32))
    later_planes = lax.fori_loop(z + 1, group_end, from_plane, none)

    @pl.when(in_group == 0)
    def _():
        st4[...] = to_fixed(
            plane_sum + plane_decay * later_planes[0], plane_decay * later_planes[1]
        )
        lax.fori_loop(0, first, send_group, 0)

    l_saved.wait()

    def factors(s, carry):
        pre = saved[s].astype(F32)
        gate_pre, up_pre = pre[:, :ff], pre[:, ff:]
        sig = 1.0 / (1.0 + jnp.exp(-gate_pre))
        fac_g[s] = up_pre * sig * (1.0 + gate_pre * (1.0 - sig))
        fac_u[s] = gate_pre * sig
        return carry

    lax.fori_loop(0, n_exp, factors, 0)

    l_w.wait()

    def expert(i):
        rcv[i, y] = snd[i, y]
        for d in range(1, n_exp):
            row_copy(i, d).wait_recv()
        got = [rcv[i, s].astype(F32) for s in range(n_exp)]
        left = jnp.concatenate([m[:cap] for m in got], axis=0)
        right = jnp.concatenate([m[cap:] for m in got], axis=0)
        arrived = jnp.concatenate([left, right], axis=1).astype(BF16)
        part = mm_nt(arrived, w[:, i * chunk:(i + 1) * chunk])
        if i == 0:
            hid[...] = part
        elif i < CHUNKS - 1:
            hid[...] += part
        else:
            part = hid[...] + part
            for s in range(n_exp):
                mine = part[s * cap:(s + 1) * cap]
                pg[s, :, :ff] = (mine * fac_g[s]).astype(BF16)
                pg[s, :, ff:] = (mine * fac_u[s]).astype(BF16)

    def from_group(at, carry):
        incoming, reach = carry
        group_copy(0, at).wait_recv()
        s, d = from_fixed(ph4[at], width)
        return incoming + reach * s, reach * d

    incoming = lax.fori_loop(group_at + 1, groups, from_group, later_planes)[0]
    for i in reversed(range(PLANE)):
        st3[i] = incoming
        if i > 0:
            s, d = parts_of(ph1, i)
            incoming = s + d * incoming
    for d in range(1, PLANE):
        plane_copy(st3, ph3, ss3, rs3, d).start()
    ph3[p] = st3[p]

    for i in range(CHUNKS - 1):
        expert(i)

    for d in range(1, PLANE):
        plane_copy(st3, ph3, ss3, rs3, d).wait_recv()
    incoming = jnp.concatenate([ph3[h] for h in range(heads)], axis=0).T
    reach = None
    for k in reversed(range(blocks)):
        here = slice(k * BLOCK, (k + 1) * BLOCK)
        if reach is None:
            carried = incoming
        else:
            carried = ls[k] + reach * incoming
        reach = decay_row[k] if reach is None else reach * decay_row[k]
        projected = mm(b[here, :], carried.astype(BF16))
        ig[here, :] = (within[here, :] + projected * endw[here, :]).astype(BF16)

    expert(CHUNKS - 1)

    for i in range(CHUNKS):
        for d in range(1, n_exp):
            row_copy(i, d).wait_send()
    for d in range(1, PLANE):
        plane_copy(st1, ph1, ss1, rs1, d).wait_send()
        plane_copy(st3, ph3, ss3, rs3, d).wait_send()

    def sent_plane(to, carry):
        z_copy(to, z).wait_send()
        return carry

    def sent_group(to, carry):
        group_copy(to, group_at).wait_send()
        return carry

    lax.fori_loop(first, z, sent_plane, 0)
    lax.fori_loop(0, lower, sent_group, 0)


def body(
    ssd_grad, in_proj_b, in_proj_c, log_decay, expert_grad, route, gate_prob, down_weight, saved_pre
):
    n_exp, n_z = lax.axis_size("exp"), lax.axis_size("ctx") // PLANE
    rows_seq, columns = ssd_grad.shape
    heads = log_decay.shape[0]
    width = columns // heads
    blocks = rows_seq // BLOCK
    state = in_proj_b.shape[1]
    rows, d_model = expert_grad.shape
    cap, ff = saved_pre.shape[3], down_weight.shape[1]
    half = d_model // CHUNKS // 2
    sizes = (n_exp, n_z, heads, width, blocks, cap, ff)
    dma = pltpu.SemaphoreType.DMA
    vmem = pltpu.VMEM
    scratch = [
        vmem((rows_seq, columns), BF16), vmem((rows_seq, state), BF16), vmem((rows_seq, state), BF16),
        vmem((heads, rows_seq), F32), vmem((rows, d_model), BF16), vmem((1, rows), jnp.int32),
        vmem((1, rows), F32), vmem((ff, d_model), BF16), vmem((n_exp, cap, 2 * ff), BF16),
        vmem((CHUNKS, n_exp, 2 * cap, half), BF16), vmem((CHUNKS, n_exp, 2 * cap, half), BF16),
        vmem((PLANE, width + EXTRA, state), F32), vmem((PLANE, width + EXTRA, state), F32),
        vmem((width + EXTRA, state), F32), vmem((n_z, width + EXTRA, state), F32),
        vmem((PLANE, width, state), F32), vmem((PLANE, width, state), F32),
        vmem((width + EXTRA16, state), I16), vmem((n_z, width + EXTRA16, state), I16),
        vmem((blocks, heads, BLOCK), F32), vmem((blocks, BLOCK, heads), F32),
        vmem((blocks, state, columns), F32), vmem((rows_seq, columns), F32),
        vmem((rows_seq, columns), F32), vmem((n_exp * cap, ff), F32),
        vmem((n_exp, cap, ff), F32), vmem((n_exp, cap, ff), F32),
        dma((9 + CHUNKS,)), dma((CHUNKS, n_exp)), dma((CHUNKS, n_exp)),
        dma((PLANE,)), dma((PLANE,)), dma((n_z,)), dma((n_z,)), dma((PLANE,)), dma((PLANE,)),
        dma((n_z,)), dma((n_z,)),
    ]
    input_grad, pre_grad = pl.pallas_call(
        functools.partial(kernel, sizes),
        out_shape=(
            jax.ShapeDtypeStruct((rows_seq, columns), BF16),
            jax.ShapeDtypeStruct((n_exp, cap, 2 * ff), BF16),
        ),
        in_specs=[pl.BlockSpec(memory_space=pltpu.HBM)] * 9,
        out_specs=(pl.BlockSpec(memory_space=pltpu.VMEM),) * 2,
        scratch_shapes=scratch,
        compiler_params=pltpu.CompilerParams(
            collective_id=0, has_side_effects=True, vmem_limit_bytes=40 * 2**20
        ),
        name="hybrid",
    )(
        *[
            pltpu.with_memory_space_constraint(operand, pltpu.HBM)
            for operand in (
                ssd_grad, in_proj_b, in_proj_c, log_decay, expert_grad, route.reshape(1, rows),
                gate_prob.reshape(1, rows), down_weight[0], saved_pre[0, 0],
            )
        ]
    )
    return input_grad, pre_grad[None, None]


def solution(mesh):
    placed = (
        P("ctx", "exp"),
        P("ctx", None),
        P("ctx", None),
        P("exp", "ctx"),
        P(("ctx", "exp"), None),
        P(("ctx", "exp"), None),
        P(("ctx", "exp")),
        P("exp", None, None),
        P("ctx", "exp", None, None, None),
    )
    return jax.shard_map(
        body,
        mesh=mesh,
        in_specs=placed,
        out_specs=(P("ctx", "exp"), P("ctx", "exp", None, None, None)),
        check_vma=False,
    )
```

```python
import functools
import math

import jax
import jax.numpy as jnp
from jax import lax
from jax.experimental import pallas as pl
from jax.experimental.pallas import tpu as pltpu
from jax.sharding import PartitionSpec as P

MESH = pl.DeviceIdType.MESH
F32, BF16, I16 = jnp.float32, jnp.bfloat16, jnp.int16
BLOCK = 256
PLANE = 8
Z_GROUP = 3
ROW_ORDER = (4, 3, 5, 2, 6, 1, 7)
CHUNKS = 4
LOG2E = math.log2(math.e)
EXTRA, EXTRA16, ONE16 = 8, 16, 14
NT = (((1,), (1,)), ((), ()))


def mm(a, b):
    return jnp.dot(a, b, preferred_element_type=F32)


def mm_nt(a, b, precision=None):
    return lax.dot_general(a, b, NT, preferred_element_type=F32, precision=precision)


def iota(shape, dim):
    return lax.broadcasted_iota(jnp.int32, shape, dim)


def decay_rows(d):
    return jnp.broadcast_to(d, (EXTRA, d.shape[1]))


def to_fixed(value, d):
    top = jnp.max(jnp.abs(value), axis=(0, 1), keepdims=True)
    power = jnp.ceil(jnp.log2(jnp.maximum(top, 1e-30)))
    power = jnp.broadcast_to(power, (1, value.shape[1]))
    coded = jnp.round(value * jnp.exp2(ONE16 - power))
    high = jnp.floor(d * 2.0**ONE16)
    low = jnp.round((d * 2.0**ONE16 - high) * 2.0**ONE16)
    row = iota((EXTRA16, value.shape[1]), 0)
    rows = jnp.where(row == 0, power, jnp.where(row == 1, high, low))
    return jnp.concatenate([coded, rows], axis=0).astype(jnp.int32).astype(jnp.int16)


def from_fixed(coded, width):
    wide = coded.astype(jnp.int32).astype(F32)
    rows = wide[width:width + 8]
    value = wide[:width] * jnp.exp2(rows[0:1] - ONE16)
    return value, (rows[1:2] + rows[2:3] * 2.0**-ONE16) * 2.0**-ONE16


def kernel(
    sizes,
    g_hbm, b_hbm, c_hbm, ld_hbm, x_hbm, route_hbm, gate_hbm, w_hbm, saved_hbm,
    ig, pg,
    g, b, c, ld, x, route, gate, w, saved,
    snd, rcv, st1, ph1, st2, ph2, st3, ph3, st4, ph4,
    cum, cumt, ls, within, endw, hid, fac_g, fac_u,
    load_sem, ss, rs, ss1, rs1, ss2, rs2, ss3, rs3, ss4, rs4, known,
):
    n_exp, n_z, heads, width, blocks, cap, ff = sizes
    state = b.shape[1]
    ctx, y = lax.axis_index("ctx"), lax.axis_index("exp")
    z, p = ctx // PLANE, lax.rem(ctx, PLANE)

    def load(i, src, dst):
        copy = pltpu.make_async_copy(src, dst, load_sem.at[i])
        copy.start()
        return copy

    barrier = pltpu.get_barrier_semaphore()

    def greet(device):
        pl.semaphore_signal(barrier, inc=1, device_id=device, device_id_type=MESH)

    speaks_later = (ctx == 0) & (y == 0)
    sends_later = (ctx == 0) & (y > 0)

    @pl.when(jnp.logical_not(speaks_later))
    def _():
        for d in ROW_ORDER:
            greet((ctx, lax.rem(y + d, n_exp)))


    l_route = load(0, route_hbm, route)
    l_gate = load(1, gate_hbm, gate)
    chunk = x.shape[1] // CHUNKS
    half = chunk // 2
    l_x = []
    for i in range(CHUNKS):
        here = slice(i * chunk, (i + 1) * chunk)
        l_x.append(load(9 + i, x_hbm.at[:, here], x.at[:, here]))

    in_group = lax.rem(z, Z_GROUP)
    first = z - in_group
    group_at = z // Z_GROUP
    group_end = jnp.minimum(first + Z_GROUP, n_z)
    groups = -(-n_z // Z_GROUP)

    def greet_plane(at, carry):
        greet((at * PLANE + p, y))
        return carry

    def greet_group(at, carry):
        greet((at * Z_GROUP * PLANE + p, y))
        return carry

    lax.fori_loop(z + 1, group_end, greet_plane, 0)
    lax.fori_loop(group_at + 1, groups, greet_group, 0)
    for d in range(1, PLANE):
        greet((z * PLANE + lax.rem(p + d, PLANE), y))

    l_ld = load(3, ld_hbm, ld)
    l_c = load(4, c_hbm, c)
    l_g = load(5, g_hbm, g)
    l_b = load(6, b_hbm, b)
    l_w = load(7, w_hbm, w)
    l_saved = load(8, saved_hbm, saved)

    rows = x.shape[0]
    slots = n_exp * cap
    l_route.wait()
    l_gate.wait()
    which = route[...]
    onehot = jnp.where(iota((n_exp, rows), 0) == which, 1.0, 0.0)
    earlier = jnp.where(iota((rows, rows), 0) < iota((rows, rows), 1), 1.0, 0.0).astype(BF16)
    before = mm(onehot.astype(BF16), earlier)
    rank = jnp.sum(before * onehot, axis=0, keepdims=True)
    slot = which * cap + rank.astype(jnp.int32)
    here = iota((slots, rows), 0) == slot
    slot_gate = jnp.sum(jnp.where(here, gate[...], 0.0), axis=1, keepdims=True)
    pick = jnp.where(here, 1.0, 0.0).astype(BF16)

    def pack(i):
        l_x[i].wait()
        part = mm(pick, x[:, i * chunk:(i + 1) * chunk]) * slot_gate
        for e in range(n_exp):
            mine = part[e * cap:(e + 1) * cap]
            both = jnp.concatenate([mine[:, :half], mine[:, half:]], axis=0)
            snd[i, e] = both.astype(BF16)

    def row_copy(i, d):
        to = lax.rem(y + d, n_exp)
        return pltpu.make_async_remote_copy(
            src_ref=snd.at[i, to], dst_ref=rcv.at[i, y],
            send_sem=ss.at[i, d], recv_sem=rs.at[i, d],
            device_id=(ctx, to), device_id_type=MESH,
        )

    pack(0)
    l_ld.wait()
    up = jnp.where(iota((BLOCK, BLOCK), 0) <= iota((BLOCK, BLOCK), 1), 1.0, 0.0)
    down = jnp.where(iota((BLOCK, BLOCK), 1) <= iota((BLOCK, BLOCK), 0), 1.0, 0.0)
    for k in range(blocks):
        steps = ld[:, k * BLOCK:(k + 1) * BLOCK]
        cum[k] = jnp.dot(steps, up, preferred_element_type=F32, precision=lax.Precision.HIGHEST)
        cumt[k] = mm_nt(down, steps, precision=lax.Precision.HIGHEST)

    lower = jnp.where(in_group == 0, z, 0)
    ring = jnp.where(sends_later, n_exp - 2, n_exp - 1)
    pl.semaphore_wait(barrier, ring + PLANE - 1 + in_group + lower)

    @pl.when(speaks_later)
    def _():
        for d in ROW_ORDER:
            to = lax.rem(y + d, n_exp)
            pl.semaphore_signal(known, inc=1, device_id=(ctx, to), device_id_type=MESH)

    def send_rows(i):
        @pl.when(jnp.logical_not(sends_later))
        def _():
            for d in ROW_ORDER:
                row_copy(i, d).start()

        @pl.when(sends_later)
        def _():
            for d in ROW_ORDER:
                @pl.when(lax.rem(y + d, n_exp) > 0)
                def _():
                    row_copy(i, d).start()

    for i in range(CHUNKS):
        if i > 0:
            pack(i)
        send_rows(i)

    columns = heads * width
    own_lane = iota((heads, columns), 1) // width == iota((heads, columns), 0)

    def spread(column):
        wide = jnp.where(own_lane, jnp.broadcast_to(column, (heads, columns)), 0.0)
        return jnp.sum(wide, axis=0, keepdims=True)

    decay = [jnp.exp(cum[k][:, BLOCK - 1:BLOCK]) for k in range(blocks)]
    decay_row = [spread(d) for d in decay]

    group = 256
    per = group // width
    lane_head = iota((BLOCK, group), 1) // width

    def own_columns(part):
        return jnp.concatenate(
            [jnp.where(lane_head == j, part, jnp.zeros_like(part)) for j in range(per)], axis=0
        )

    l_c.wait()
    l_g.wait()
    eye = jnp.where(iota((state, state), 0) == iota((state, state), 1), 1.0, 0.0).astype(BF16)

    def local(k, carry):
        at = pl.multiple_of(k * BLOCK, BLOCK)
        ct = mm_nt(eye, c[pl.ds(at, BLOCK), :])
        grown = jnp.exp(cum[k])
        for q in range(heads // per):
            left = jnp.concatenate(
                [(ct * grown[q * per + j:q * per + j + 1, :]).astype(BF16) for j in range(per)],
                axis=1,
            )
            right = own_columns(g[pl.ds(at, BLOCK), q * group:(q + 1) * group])
            ls[k, :, q * group:(q + 1) * group] = mm(left, right)
        return carry

    lax.fori_loop(0, blocks, local, 0)

    total = ls[blocks - 1]
    for k in reversed(range(blocks - 1)):
        inner = total
        total = ls[k] + decay_row[k] * inner
        ls[k] = inner
    whole_decay = decay[0]
    for k in range(1, blocks):
        whole_decay = whole_decay * decay[k]
    total_t = total.T
    wide_decay = jnp.broadcast_to(whole_decay, (heads, state))
    for h in range(heads):
        st1[h, :width, :] = total_t[h * width:(h + 1) * width, :]
        st1[h, width:, :] = decay_rows(wide_decay[h:h + 1, :])

    def plane_copy(src, dst, s_sem, r_sem, d):
        to = lax.rem(p + d, PLANE)
        return pltpu.make_async_remote_copy(
            src_ref=src.at[to], dst_ref=dst.at[p],
            send_sem=s_sem.at[d], recv_sem=r_sem.at[d],
            device_id=(z * PLANE + to, y), device_id_type=MESH,
        )

    for d in range(1, PLANE):
        plane_copy(st1, ph1, ss1, rs1, d).start()
    ph1[p] = st1[p]

    l_b.wait()
    later = iota((BLOCK, BLOCK), 1) >= iota((BLOCK, BLOCK), 0)

    def inside(k, carry):
        at = pl.multiple_of(k * BLOCK, BLOCK)
        scores = mm_nt(b[pl.ds(at, BLOCK), :], c[pl.ds(at, BLOCK), :])
        scores = jnp.where(later, scores, 0.0)
        across = cum[k] * LOG2E
        along = cumt[k] * LOG2E
        for q in range(heads // per):
            parts = []
            for j in range(per):
                h = q * per + j
                gap = jnp.minimum(across[h:h + 1, :] - along[:, h:h + 1], 0.0)
                parts.append((scores * jnp.exp2(gap)).astype(BF16))
            left = jnp.concatenate(parts, axis=1)
            right = own_columns(g[pl.ds(at, BLOCK), q * group:(q + 1) * group])
            within[pl.ds(at, BLOCK), q * group:(q + 1) * group] = mm(left, right)
        rest = jnp.exp2(along[BLOCK - 1:BLOCK, :] - along)
        first = iota((BLOCK, 2 * width), 1) < width
        for q in range(heads // 2):
            endw[pl.ds(at, BLOCK), q * 2 * width:(q + 1) * 2 * width] = jnp.where(
                first, rest[:, 2 * q:2 * q + 1], rest[:, 2 * q + 1:2 * q + 2]
            )
        return carry

    lax.fori_loop(0, blocks, inside, 0)

    @pl.when(sends_later)
    def _():
        pl.semaphore_wait(known, 1)
        for i in range(CHUNKS):
            row_copy(i, n_exp - y).start()

    for d in range(1, PLANE):
        plane_copy(st1, ph1, ss1, rs1, d).wait_recv()

    def parts_of(ref, at):
        return (
            ref[at, :width, :],
            ref[at, width:width + 1, :],
        )

    plane_sum, plane_decay = parts_of(ph1, PLANE - 1)
    for i in reversed(range(PLANE - 1)):
        s, d = parts_of(ph1, i)
        plane_sum = s + d * plane_sum
        plane_decay = plane_decay * d
    st2[:width, :] = plane_sum
    st2[width:, :] = decay_rows(plane_decay)

    def z_copy(to, at):
        return pltpu.make_async_remote_copy(
            src_ref=st2, dst_ref=ph2.at[at],
            send_sem=ss2.at[to], recv_sem=rs2.at[at],
            device_id=(to * PLANE + p, y), device_id_type=MESH,
        )

    def group_copy(to, at):
        return pltpu.make_async_remote_copy(
            src_ref=st4, dst_ref=ph4.at[at],
            send_sem=ss4.at[to], recv_sem=rs4.at[at],
            device_id=(to * PLANE + p, y), device_id_type=MESH,
        )

    def send_plane(to, carry):
        z_copy(to, z).start()
        return carry

    def send_group(to, carry):
        group_copy(to, group_at).start()
        return carry

    lax.fori_loop(first, z, send_plane, 0)

    def from_plane(at, carry):
        incoming, reach = carry
        z_copy(0, at).wait_recv()
        s, d = parts_of(ph2, at)
        return incoming + reach * s, reach * d

    none = (jnp.zeros((width, state), F32), jnp.ones((1, state), F32))
    later_planes = lax.fori_loop(z + 1, group_end, from_plane, none)

    @pl.when(in_group == 0)
    def _():
        st4[...] = to_fixed(
            plane_sum + plane_decay * later_planes[0], plane_decay * later_planes[1]
        )
        lax.fori_loop(0, first, send_group, 0)

    l_saved.wait()

    def factors(s, carry):
        pre = saved[s].astype(F32)
        gate_pre, up_pre = pre[:, :ff], pre[:, ff:]
        sig = 1.0 / (1.0 + jnp.exp(-gate_pre))
        fac_g[s] = up_pre * sig * (1.0 + gate_pre * (1.0 - sig))
        fac_u[s] = gate_pre * sig
        return carry

    lax.fori_loop(0, n_exp, factors, 0)

    l_w.wait()

    def expert(i):
        rcv[i, y] = snd[i, y]
        for d in range(1, n_exp):
            row_copy(i, d).wait_recv()
        got = [rcv[i, s].astype(F32) for s in range(n_exp)]
        left = jnp.concatenate([m[:cap] for m in got], axis=0)
        right = jnp.concatenate([m[cap:] for m in got], axis=0)
        arrived = jnp.concatenate([left, right], axis=1).astype(BF16)
        part = mm_nt(arrived, w[:, i * chunk:(i + 1) * chunk])
        if i == 0:
            hid[...] = part
        elif i < CHUNKS - 1:
            hid[...] += part
        else:
            part = hid[...] + part
            for s in range(n_exp):
                mine = part[s * cap:(s + 1) * cap]
                pg[s, :, :ff] = (mine * fac_g[s]).astype(BF16)
                pg[s, :, ff:] = (mine * fac_u[s]).astype(BF16)

    def from_group(at, carry):
        incoming, reach = carry
        group_copy(0, at).wait_recv()
        s, d = from_fixed(ph4[at], width)
        return incoming + reach * s, reach * d

    incoming = lax.fori_loop(group_at + 1, groups, from_group, later_planes)[0]
    for i in reversed(range(PLANE)):
        st3[i] = incoming
        if i > 0:
            s, d = parts_of(ph1, i)
            incoming = s + d * incoming
    for d in range(1, PLANE):
        plane_copy(st3, ph3, ss3, rs3, d).start()
    ph3[p] = st3[p]

    for i in range(CHUNKS - 1):
        expert(i)

    for d in range(1, PLANE):
        plane_copy(st3, ph3, ss3, rs3, d).wait_recv()
    incoming = jnp.concatenate([ph3[h] for h in range(heads)], axis=0).T
    reach = None
    for k in reversed(range(blocks)):
        here = slice(k * BLOCK, (k + 1) * BLOCK)
        if reach is None:
            carried = incoming
        else:
            carried = ls[k] + reach * incoming
        reach = decay_row[k] if reach is None else reach * decay_row[k]
        projected = mm(b[here, :], carried.astype(BF16))
        ig[here, :] = (within[here, :] + projected * endw[here, :]).astype(BF16)

    expert(CHUNKS - 1)

    for i in range(CHUNKS):
        for d in range(1, n_exp):
            row_copy(i, d).wait_send()
    for d in range(1, PLANE):
        plane_copy(st1, ph1, ss1, rs1, d).wait_send()
        plane_copy(st3, ph3, ss3, rs3, d).wait_send()

    def sent_plane(to, carry):
        z_copy(to, z).wait_send()
        return carry

    def sent_group(to, carry):
        group_copy(to, group_at).wait_send()
        return carry

    lax.fori_loop(first, z, sent_plane, 0)
    lax.fori_loop(0, lower, sent_group, 0)


def body(
    ssd_grad, in_proj_b, in_proj_c, log_decay, expert_grad, route, gate_prob, down_weight, saved_pre
):
    n_exp, n_z = lax.axis_size("exp"), lax.axis_size("ctx") // PLANE
    rows_seq, columns = ssd_grad.shape
    heads = log_decay.shape[0]
    width = columns // heads
    blocks = rows_seq // BLOCK
    state = in_proj_b.shape[1]
    rows, d_model = expert_grad.shape
    cap, ff = saved_pre.shape[3], down_weight.shape[1]
    half = d_model // CHUNKS // 2
    sizes = (n_exp, n_z, heads, width, blocks, cap, ff)
    dma = pltpu.SemaphoreType.DMA
    vmem = pltpu.VMEM
    scratch = [
        vmem((rows_seq, columns), BF16), vmem((rows_seq, state), BF16), vmem((rows_seq, state), BF16),
        vmem((heads, rows_seq), F32), vmem((rows, d_model), BF16), vmem((1, rows), jnp.int32),
        vmem((1, rows), F32), vmem((ff, d_model), BF16), vmem((n_exp, cap, 2 * ff), BF16),
        vmem((CHUNKS, n_exp, 2 * cap, half), BF16), vmem((CHUNKS, n_exp, 2 * cap, half), BF16),
        vmem((PLANE, width + EXTRA, state), F32), vmem((PLANE, width + EXTRA, state), F32),
        vmem((width + EXTRA, state), F32), vmem((n_z, width + EXTRA, state), F32),
        vmem((PLANE, width, state), F32), vmem((PLANE, width, state), F32),
        vmem((width + EXTRA16, state), I16), vmem((n_z, width + EXTRA16, state), I16),
        vmem((blocks, heads, BLOCK), F32), vmem((blocks, BLOCK, heads), F32),
        vmem((blocks, state, columns), F32), vmem((rows_seq, columns), F32),
        vmem((rows_seq, columns), F32), vmem((n_exp * cap, ff), F32),
        vmem((n_exp, cap, ff), F32), vmem((n_exp, cap, ff), F32),
        dma((9 + CHUNKS,)), dma((CHUNKS, n_exp)), dma((CHUNKS, n_exp)),
        dma((PLANE,)), dma((PLANE,)), dma((n_z,)), dma((n_z,)), dma((PLANE,)), dma((PLANE,)),
        dma((n_z,)), dma((n_z,)), pltpu.SemaphoreType.REGULAR,
    ]
    input_grad, pre_grad = pl.pallas_call(
        functools.partial(kernel, sizes),
        out_shape=(
            jax.ShapeDtypeStruct((rows_seq, columns), BF16),
            jax.ShapeDtypeStruct((n_exp, cap, 2 * ff), BF16),
        ),
        in_specs=[pl.BlockSpec(memory_space=pltpu.HBM)] * 9,
        out_specs=(pl.BlockSpec(memory_space=pltpu.VMEM),) * 2,
        scratch_shapes=scratch,
        compiler_params=pltpu.CompilerParams(
            collective_id=0, has_side_effects=True, vmem_limit_bytes=40 * 2**20
        ),
        name="hybrid",
    )(
        *[
            pltpu.with_memory_space_constraint(operand, pltpu.HBM)
            for operand in (
                ssd_grad, in_proj_b, in_proj_c, log_decay, expert_grad, route.reshape(1, rows),
                gate_prob.reshape(1, rows), down_weight[0], saved_pre[0, 0],
            )
        ]
    )
    return input_grad, pre_grad[None, None]


def solution(mesh):
    placed = (
        P("ctx", "exp"),
        P("ctx", None),
        P("ctx", None),
        P("exp", "ctx"),
        P(("ctx", "exp"), None),
        P(("ctx", "exp"), None),
        P(("ctx", "exp")),
        P("exp", None, None),
        P("ctx", "exp", None, None, None),
    )
    return jax.shard_map(
        body,
        mesh=mesh,
        in_specs=placed,
        out_specs=(P("ctx", "exp"), P("ctx", "exp", None, None, None)),
        check_vma=False,
    )
```
